256 devices in a mesh: section: 32 (over x, z_hi, y), tensor: 8 (over z_lo, core).
Axes of the slice: x: 4, y: 4, z: 8 (z_hi: 2, z_lo: 4; z = z_hi * 4 + z_lo), core: 2. Of those that a mesh axis runs over, the one named last changes fastest.
Arguments:
- down_terms: bfloat16 [32, 8, 128, 16384], P('section', 'tensor'), may hold values from -6 to 6
- residual: bfloat16 [32, 128, 16384], P('section', 'tensor'), may hold values from -6 to 6
- norm_gain: bfloat16 [32, 16384], P('section'), may hold values from 0.099609375 to 1.8984375
- kv_weight: bfloat16 [32, 16384, 2048], P('section', None, 'tensor'), may hold values from -0.046875 to 0.046875
Outputs:
- keys_values: bfloat16 [32, 128, 2048], P('section', None, 'tensor')
The draws below stay inside these ranges and needn't reach their ends.
All inputs are finite; a program needn't handle non-finite values.
Results may differ from the reference program's by a relative error of at most 0.02.
Values may be sent and summed in bfloat16 or wider, within the bound.
A program may use at most 64 MiB of HBM per device.

```python
import jax
import jax.numpy as jnp
from jax import lax

D = 16384
KV = 2048
TOKENS = 128
N_SECTION = 32
N_TENSOR = 8


def spiked(values, key, source, target, parts, factor):
    def block_of(position):
        return (jnp.arange(values.shape[position]) // (values.shape[position] // parts)).reshape((-1,) + (1,) * (values.ndim - 1 - position))

    near = jax.random.permutation(key, parts)[block_of(target)]
    other_side = (block_of(target) + parts // 2) % parts
    return jnp.where((block_of(source) == near) | (block_of(source) == other_side), factor * values, values)


def block_scale(key, extent, shards, low, top_value):
    loudness = 1.0
    for position, shards_of in shards:
        heights = jax.random.uniform(jax.random.fold_in(jax.random.fold_in(key, 6), position), (shards_of,), jnp.float32, low / len(shards), top_value / len(shards))
        loudness = loudness * jnp.repeat(jnp.exp(heights), extent[position] // shards_of).reshape((-1,) + (1,) * (len(extent) - 1 - position))
    return loudness


def noise(key, dims, scale, bound, cuts=(), dtype=jnp.bfloat16):
    result = jax.random.normal(key, dims, jnp.float32) * scale
    if len(cuts) > 0:
        result = block_scale(key, dims, cuts, -0.22, 0.18) * result
    return jnp.clip(result, min=-bound, max=bound).astype(dtype)


def noise_with(own_key, shape, width, reach, pieces, heavy, kind=jnp.bfloat16):
    entries = width * jax.random.normal(own_key, shape, jnp.float32)
    if pieces:
        entries = entries * block_scale(own_key, shape, pieces, -0.22, 0.18)
    return jnp.clip(spiked(entries, jax.random.fold_in(own_key, 3), *heavy), -reach, reach).astype(kind)


def setup_inputs(seed: int = 0) -> dict:
    keys = jax.random.split(jax.random.key(seed), 5)
    down_terms = noise_with(keys[0], (N_SECTION, N_TENSOR, TOKENS, D), 0.5, 6.0, ((0, 32), (1, 8)), (1, 2, 8, 2.0))
    residual = noise(keys[1], (N_SECTION, TOKENS, D), 1.0, 6.0, ((0, 32), (1, 8)))
    norm_gain = jnp.clip(1.0 + 0.18 * jax.random.normal(keys[2], (N_SECTION, D), jnp.float32), 0.099609375, 1.8984375).astype(jnp.bfloat16)
    kv_weight = noise(keys[3], (N_SECTION, D, KV), D ** -0.5, 0.046875, ((0, 32), (2, 8)))
    return {"down_terms": down_terms, "residual": residual, "norm_gain": norm_gain, "kv_weight": kv_weight}


def section_normed(items):
    terms_one, residual_one, gain_one = items
    mixed = lax.optimization_barrier(jnp.sum(terms_one.astype(jnp.float32), axis=0))
    stream = residual_one.astype(jnp.float32) + mixed
    scale = lax.rsqrt(lax.optimization_barrier(jnp.mean(stream * stream, axis=1, keepdims=True)) + 1e-05)
    return (stream * scale * gain_one.astype(jnp.float32)[None, :]).astype(jnp.bfloat16)

def section_project(pair):
    arrived, weight_one = pair
    return jnp.dot(arrived, weight_one, preferred_element_type=jnp.float32).astype(jnp.bfloat16)

def reference(down_terms, residual, norm_gain, kv_weight):
    normed = lax.map(section_normed, (down_terms, residual, norm_gain))
    arrived = jnp.roll(normed, 1, axis=0)
    return lax.map(section_project, (arrived, kv_weight))
```

```python
import jax
import jax.numpy as jnp
from jax import lax
from jax.sharding import PartitionSpec as P


def passed_along(array, axis, by):
    devices = lax.axis_size(axis)
    return lax.ppermute(array, axis, [(i, (i + by) % devices) for i in range(devices)])


def body(down_terms, residual, norm_gain, kv_weight):
    own_terms = down_terms[0, 0]
    stream_rows = residual[0]
    gain_row = norm_gain[0].astype(jnp.float32)
    kv_cols = kv_weight[0]
    mixed = lax.psum_scatter(
        own_terms.astype(jnp.float32).astype(jnp.bfloat16),
        "tensor",
        scatter_dimension=0,
        tiled=True,
    ).astype(jnp.float32)
    stream = stream_rows.astype(jnp.float32) + mixed
    scale = lax.rsqrt(jnp.mean(stream * stream, axis=1, keepdims=True) + 1e-05)
    normed = (stream * scale * gain_row[None, :]).astype(jnp.bfloat16)
    hopped = passed_along(normed, "section", 1)
    arrived = lax.all_gather(hopped, "tensor", axis=0, tiled=True)
    result = jnp.dot(arrived, kv_cols, preferred_element_type=jnp.float32)
    return result.astype(jnp.bfloat16)[None]


def solution(mesh):
    in_specs = (
        P("section", "tensor", None, None),
        P("section", "tensor", None),
        P("section", None),
        P("section", None, "tensor"),
    )
    out_specs = P("section", None, "tensor")
    return jax.shard_map(body, mesh=mesh, in_specs=in_specs, out_specs=out_specs, check_vma=False)
```

```python
import functools

import jax
import jax.numpy as jnp
from jax import lax
from jax.experimental import pallas as pl
from jax.experimental.pallas import tpu as pltpu
from jax.sharding import PartitionSpec as P

MESH = pl.DeviceIdType.MESH
BF16, F32 = jnp.bfloat16, jnp.float32

Y_RUN = 4
CHUNKS = 16
EDGE_SKEW = (0, 3, 4, 7, 8)
MID_SKEW = (1, 2, 5, 6, 8)


def kernel(n_section, down, res, gain, weight, out,
           own, pair, resv, gainv, wv, sent, got, x, scale_out, scales, acc, squares,
           own_sem, res_sem, gain_sem, w_sem, pair_recv, got_recv, x_recv, scale_recv, send_sem):
    chunks, _, rows, width = own.shape
    section, tensor = lax.axis_index("section"), lax.axis_index("tensor")
    z, core = tensor // 2, tensor % 2
    near = z // 2
    far = 1 - near
    is_edge = z % 3 == 0
    is_mid = z % 3 != 0
    inward = z + 1 - 2 * near
    outward = z - 1 + 2 * near
    flip_out = (section % Y_RUN) // (Y_RUN - 1)
    flip_in = 1 - (section % Y_RUN + Y_RUN - 1) // Y_RUN
    next_section = (section + 1) % n_section
    prev_section = (section + n_section - 1) % n_section
    next_near = (near + flip_out) % 2

    sibling_id = (section, z * 2 + 1 - core)
    inward_id = (section, inward * 2 + core)
    outward_id = (section, outward * 2 + core)
    next_id = (next_section, next_near * 6 + core)
    prev_id = (prev_section, ((near + flip_in) % 2) * 6 + core)

    def remote(src, dst, kind, recv, device):
        return pltpu.make_async_remote_copy(
            src_ref=src, dst_ref=dst, send_sem=send_sem.at[kind], recv_sem=recv, device_id=device, device_id_type=MESH
        )

    def cols(k):
        return pl.ds(pl.multiple_of(k * width, width), width)

    def own_copy(k):
        return pltpu.make_async_copy(down.at[:, core, :, cols(k)], own.at[k], own_sem.at[k])

    def res_copy(k):
        return pltpu.make_async_copy(res.at[:, cols(k)], resv.at[k], res_sem.at[k])

    def w_copy(k):
        return pltpu.make_async_copy(weight.at[cols(k)], wv.at[k], w_sem.at[k])

    def pair_copy(k):
        return remote(down.at[:, 1 - core, :, cols(k)], pair.at[k], 0, pair_recv.at[k], sibling_id)

    def got_copy(k, lane, kind, device):
        return remote(sent.at[lane, k], got.at[lane, k], kind, got_recv.at[lane, k], device)

    def part(of, flow):
        return pl.ds(of * 4 + flow * 2, 2)

    def hop_copy(k):
        return remote(sent.at[near, k], x.at[k, part(core, next_near)], 2, x_recv.at[core, next_near, k], next_id)

    def x_copy(k, of, flow, kind, device):
        return remote(x.at[k, part(of, flow)], x.at[k, part(of, flow)], kind, x_recv.at[of, flow, k], device)

    def scale_copy(of, flow, kind, device):
        return remote(scales.at[of, flow], scales.at[of, flow], kind, scale_recv.at[of, flow], device)

    gain_copy = pltpu.make_async_copy(gain, gainv, gain_sem)

    @pl.loop(0, chunks)
    def _(k):
        own_copy(k).start()

    gain_copy.start()

    barrier = pltpu.get_barrier_semaphore()

    def greet(device):
        pl.semaphore_signal(barrier, inc=1, device_id=device, device_id_type=MESH)

    greet(sibling_id)
    greet(inward_id)

    @pl.when(is_edge)
    def _():
        greet(next_id)
        greet(prev_id)
        pl.semaphore_wait(barrier, 4)

    @pl.when(is_mid)
    def _():
        greet(outward_id)
        pl.semaphore_wait(barrier, 3)

    @pl.loop(0, chunks)
    def _(k):
        pair_copy(k).start()

    @pl.loop(0, chunks)
    def _(k):
        res_copy(k).start()

    @pl.loop(0, chunks)
    def _(k):
        w_copy(k).start()

    acc[...] = jnp.zeros_like(acc)
    squares[...] = jnp.zeros_like(squares)
    gain_copy.wait()

    def partial_sum(k, lane, sub):
        index = lane * 2 + sub
        return own[k, index].astype(F32) + pair[k, index].astype(F32)

    def at(i, skew, body):
        k = i - skew

        @pl.when((k >= 0) & (k < chunks))
        def _():
            body(k)

    def arrived(k):
        own_copy(k).wait()
        pair_copy(k).wait_recv()

    def edge_far_reduce(k):
        arrived(k)
        for sub in range(2):
            sent[far, k, sub] = partial_sum(k, far, sub).astype(BF16)
        got_copy(k, far, 1, inward_id).start()

    def mid_far_reduce(k):
        arrived(k)
        got_copy(k, far, 1, inward_id).wait_recv()
        for sub in range(2):
            sent[far, k, sub] = (got[far, k, sub].astype(F32) + partial_sum(k, far, sub)).astype(BF16)
        got_copy(k, far, 1, inward_id).start()

    def near_sum(k, sub):
        mask = ((sub + z + 1) % 2).astype(F32)
        return got[near, k, sub].astype(F32) + partial_sum(k, near, sub) + resv[k].astype(F32) * mask

    def edge_near_reduce(k):
        res_copy(k).wait()
        got_copy(k, near, 1, inward_id).wait_recv()
        gain_row = gainv[:, cols(k)].astype(F32)
        for sub in range(2):
            stream = near_sum(k, sub)
            square = stream * stream
            folded = square[:, :128]
            for j in range(1, width // 128):
                folded = folded + square[:, j * 128:(j + 1) * 128]
            squares[sub] += folded
            sent[near, k, sub] = (stream * gain_row).astype(BF16)
        hop_copy(k).start()

        @pl.when(k == chunks - 1)
        def _():
            total = jnp.sum(squares[...], axis=2, keepdims=True) * (1.0 / (chunks * width))
            scale_out[...] = jnp.broadcast_to(lax.rsqrt(total + 1e-05), scale_out.shape)
            remote(scale_out, scales.at[core, next_near], 7, scale_recv.at[core, next_near], next_id).start()

    def mid_near_reduce(k):
        res_copy(k).wait()
        got_copy(k, near, 1, inward_id).wait_recv()
        for sub in range(2):
            sent[near, k, sub] = near_sum(k, sub).astype(BF16)
        got_copy(k, near, 2, outward_id).start()

    def near_spread(k):
        x_copy(k, core, near, 3, inward_id).wait_recv()
        x_copy(k, core, near, 3, inward_id).start()
        x_copy(k, core, near, 4, sibling_id).start()

        @pl.when(k == chunks - 1)
        def _():
            scale_copy(core, near, 8, inward_id).wait_recv()
            scale_copy(core, near, 8, inward_id).start()
            scale_copy(core, near, 9, sibling_id).start()

    def far_spread(k):
        x_copy(k, core, far, 6, sibling_id).wait_recv()

        @pl.when(is_mid)
        def _():
            x_copy(k, core, far, 5, outward_id).start()

        x_copy(k, core, far, 6, sibling_id).start()

        @pl.when(k == chunks - 1)
        def _():
            scale_copy(core, far, 11, sibling_id).wait_recv()

            @pl.when(is_mid)
            def _():
                scale_copy(core, far, 10, outward_id).start()

            scale_copy(core, far, 11, sibling_id).start()

    def product(k):
        w_copy(k).wait()
        for flow in range(2):
            x_copy(k, 1 - core, flow, 4, sibling_id).wait_recv()
        acc[...] += jnp.dot(x[k].reshape(8 * rows, width), wv[k], preferred_element_type=F32)

    @pl.when(is_edge)
    def _():
        @pl.loop(0, chunks + max(EDGE_SKEW))
        def _(i):
            at(i, EDGE_SKEW[0], edge_far_reduce)
            at(i, EDGE_SKEW[1], edge_near_reduce)
            at(i, EDGE_SKEW[2], near_spread)
            at(i, EDGE_SKEW[3], far_spread)
            at(i, EDGE_SKEW[4], product)

    @pl.when(is_mid)
    def _():
        @pl.loop(0, chunks + max(MID_SKEW))
        def _(i):
            at(i, MID_SKEW[0], mid_far_reduce)
            at(i, MID_SKEW[1], mid_near_reduce)
            at(i, MID_SKEW[2], near_spread)
            at(i, MID_SKEW[3], far_spread)
            at(i, MID_SKEW[4], product)

    for flow in range(2):
        scale_copy(1 - core, flow, 9, sibling_id).wait_recv()
    lane_of = (flip_in, 1 - flip_in)
    for of in range(2):
        for flow in range(2):
            for sub in range(2):
                start = (of * 4 + flow * 2 + sub) * rows
                factor = scales[of, flow, sub]
                block = acc[start:start + rows] * jnp.concatenate([factor, factor], axis=1)
                out[lane_of[flow] * 2 + sub, of] = block.astype(BF16)

    def sent_all(ref, kind):
        remote(ref, ref, kind, pair_recv.at[0], sibling_id).wait_send()

    sent_all(down.at[:, 1 - core], 0)
    sent_all(sent.at[far], 1)
    sent_all(sent.at[near], 2)
    sent_all(x.at[:, part(core, near)], 3)
    sent_all(x.at[:, part(core, near)], 4)
    sent_all(x.at[:, part(core, far)], 6)
    sent_all(scales.at[core, near], 8)
    sent_all(scales.at[core, near], 9)
    sent_all(scales.at[core, far], 11)

    @pl.when(is_edge)
    def _():
        sent_all(scale_out, 7)

    @pl.when(is_mid)
    def _():
        sent_all(x.at[:, part(core, far)], 5)
        sent_all(scales.at[core, far], 10)


def body(n_section, down_terms, residual, norm_gain, kv_weight):
    tokens, d = down_terms.shape[2:]
    kv = kv_weight.shape[2]
    rows, chunks = tokens // 8, CHUNKS
    width = d // chunks
    anywhere = pl.BlockSpec(memory_space=pl.ANY)
    out = pl.pallas_call(
        functools.partial(kernel, n_section),
        out_shape=jax.ShapeDtypeStruct((4, 2, rows, kv), BF16),
        in_specs=[anywhere] * 4,
        out_specs=pl.BlockSpec(memory_space=pltpu.VMEM),
        scratch_shapes=[
            pltpu.VMEM((chunks, 4, rows, width), BF16),
            pltpu.VMEM((chunks, 4, rows, width), BF16),
            pltpu.VMEM((chunks, rows, width), BF16),
            pltpu.VMEM((1, d), BF16),
            pltpu.VMEM((chunks, width, kv), BF16),
            pltpu.VMEM((2, chunks, 2, rows, width), BF16),
            pltpu.VMEM((2, chunks, 2, rows, width), BF16),
            pltpu.VMEM((chunks, 8, rows, width), BF16),
            pltpu.VMEM((2, rows, 128), F32),
            pltpu.VMEM((2, 2, 2, rows, 128), F32),
            pltpu.VMEM((tokens, kv), F32),
            pltpu.VMEM((2, rows, 128), F32),
            pltpu.SemaphoreType.DMA((chunks,)),
            pltpu.SemaphoreType.DMA((chunks,)),
            pltpu.SemaphoreType.DMA,
            pltpu.SemaphoreType.DMA((chunks,)),
            pltpu.SemaphoreType.DMA((chunks,)),
            pltpu.SemaphoreType.DMA((2, chunks)),
            pltpu.SemaphoreType.DMA((2, 2, chunks)),
            pltpu.SemaphoreType.DMA((2, 2)),
            pltpu.SemaphoreType.DMA((12,)),
        ],
        compiler_params=pltpu.CompilerParams(
            collective_id=0, has_side_effects=True, vmem_limit_bytes=48 * 1024 * 1024
        ),
        cost_estimate=pl.CostEstimate(flops=2 * tokens * d * kv, bytes_accessed=13 * 2**20, transcendentals=0),
    )(
        down_terms.reshape(4, 2, rows, d),
        residual.reshape(rows, d),
        norm_gain,
        kv_weight.reshape(d, kv),
    )
    return out.reshape(1, tokens, kv)


def solution(mesh):
    in_specs = (
        P("section", "tensor", None, None),
        P("section", "tensor", None),
        P("section", None),
        P("section", None, "tensor"),
    )
    out_specs = P("section", None, "tensor")
    return jax.shard_map(
        functools.partial(body, mesh.shape["section"]), mesh=mesh, in_specs=in_specs, out_specs=out_specs, check_vma=False
    )
```

```python
import functools

import jax
import jax.numpy as jnp
from jax import lax
from jax.experimental import pallas as pl
from jax.experimental.pallas import tpu as pltpu
from jax.sharding import PartitionSpec as P

MESH = pl.DeviceIdType.MESH
BF16, F32 = jnp.bfloat16, jnp.float32

Y_RUN = 4
CHUNKS = 16
EDGE_SKEW = (0, 6, 14, 23, 26)
MID_SKEW = (2, 4, 17, 20, 26)


def kernel(n_section, down, res, gain, weight, out,
           own, pair, resv, gainv, wv, sent, got, x, scale_out, scales, acc, squares,
           own_sem, res_sem, gain_sem, w_sem, pair_recv, got_recv, x_recv, sibling_recv, scale_recv, send_sem, line_sem):
    chunks, _, rows, width = own.shape
    section, tensor = lax.axis_index("section"), lax.axis_index("tensor")
    z, core = tensor // 2, tensor % 2
    near = z // 2
    far = 1 - near
    is_edge = z % 3 == 0
    is_mid = z % 3 != 0
    inward = z + 1 - 2 * near
    outward = z - 1 + 2 * near
    flip_out = (section % Y_RUN) // (Y_RUN - 1)
    flip_in = 1 - (section % Y_RUN + Y_RUN - 1) // Y_RUN
    next_section = (section + 1) % n_section
    prev_section = (section + n_section - 1) % n_section
    next_near = (near + flip_out) % 2

    sibling_id = (section, z * 2 + 1 - core)
    inward_id = (section, inward * 2 + core)
    outward_id = (section, outward * 2 + core)
    next_id = (next_section, next_near * 6 + core)
    prev_id = (prev_section, ((near + flip_in) % 2) * 6 + core)

    def remote(src, dst, kind, recv, device):
        return pltpu.make_async_remote_copy(
            src_ref=src, dst_ref=dst, send_sem=send_sem.at[kind], recv_sem=recv, device_id=device, device_id_type=MESH
        )

    def cols(k):
        return pl.ds(pl.multiple_of(k * width, width), width)

    def own_copy(k):
        return pltpu.make_async_copy(down.at[:, core, :, cols(k)], own.at[k], own_sem.at[k])

    def res_copy(k):
        return pltpu.make_async_copy(res.at[:, cols(k)], resv.at[k], res_sem.at[k])

    def w_copy(k):
        return pltpu.make_async_copy(weight.at[cols(k)], wv.at[k], w_sem.at[k])

    def pair_copy(k):
        return remote(down.at[:, 1 - core, :, cols(k)], pair.at[k], 0, pair_recv.at[k], sibling_id)

    def got_copy(k, lane, kind, device):
        return remote(sent.at[lane, k], got.at[lane, k], kind, got_recv.at[lane, k], device)

    def part(of, flow):
        return pl.ds(of * 4 + flow * 2, 2)

    def hop_copy(k):
        return remote(sent.at[near, k], x.at[k, part(core, next_near)], 2, x_recv.at[next_near, k], next_id)

    def x_copy(k, of, flow, kind, device):
        return remote(x.at[k, part(of, flow)], x.at[k, part(of, flow)], kind, x_recv.at[flow, k], device)

    def both_copy(k):
        mine = x.at[k, pl.ds(core * 4, 4)]
        return remote(mine, mine, 4, sibling_recv.at[k], sibling_id)

    def scale_copy(of, flow, kind, device):
        return remote(scales.at[of, flow], scales.at[of, flow], kind, scale_recv.at[of, flow], device)

    gain_copy = pltpu.make_async_copy(gain, gainv, gain_sem)

    barrier = pltpu.get_barrier_semaphore()

    def greet(device):
        pl.semaphore_signal(barrier, inc=1, device_id=device, device_id_type=MESH)

    @pl.when(is_edge)
    def _():
        greet(inward_id)
        greet((section, inward * 2 + 1 - core))
        greet(prev_id)

    @pl.when(is_mid)
    def _():
        greet(sibling_id)
        greet(inward_id)

    @pl.loop(0, chunks)
    def _(k):
        own_copy(k).start()

    gain_copy.start()

    @pl.loop(0, chunks)
    def _(k):
        res_copy(k).start()

    @pl.when(is_mid)
    def _():
        pl.semaphore_wait(barrier, 4)
        pl.semaphore_signal(line_sem, inc=1, device_id=outward_id, device_id_type=MESH)

    @pl.when(is_edge)
    def _():
        pl.semaphore_wait(line_sem, 1)

    @pl.loop(0, chunks)
    def _(k):
        pair_copy(k).start()

    acc[...] = jnp.zeros_like(acc)
    squares[...] = jnp.zeros_like(squares)

    def partial_sum(k, lane, sub):
        index = lane * 2 + sub
        return own[k, index].astype(F32) + pair[k, index].astype(F32)

    def at(i, skew, body):
        k = i - skew

        @pl.when((k >= 0) & (k < chunks))
        def _():
            body(k)

    def arrived(k):
        own_copy(k).wait()
        pair_copy(k).wait_recv()

    def edge_far_reduce(k):
        arrived(k)
        for sub in range(2):
            sent[far, k, sub] = partial_sum(k, far, sub).astype(BF16)
        got_copy(k, far, 1, inward_id).start()

    def mid_far_reduce(k):
        arrived(k)
        got_copy(k, far, 1, inward_id).wait_recv()
        for sub in range(2):
            sent[far, k, sub] = (got[far, k, sub].astype(F32) + partial_sum(k, far, sub)).astype(BF16)
        got_copy(k, far, 1, inward_id).start()

    def near_sum(k, sub):
        mask = ((sub + z + 1) % 2).astype(F32)
        return got[near, k, sub].astype(F32) + partial_sum(k, near, sub) + resv[k].astype(F32) * mask

    def edge_near_reduce(k):
        w_copy(k).start()
        @pl.when(k == 0)
        def _():
            gain_copy.wait()
            pl.semaphore_wait(barrier, 1)

        res_copy(k).wait()
        got_copy(k, near, 1, inward_id).wait_recv()
        gain_row = gainv[:, cols(k)].astype(F32)
        for sub in range(2):
            stream = near_sum(k, sub)
            square = stream * stream
            folded = square[:, :128]
            for j in range(1, width // 128):
                folded = folded + square[:, j * 128:(j + 1) * 128]
            squares[sub] += folded
            sent[near, k, sub] = (stream * gain_row).astype(BF16)
        hop_copy(k).start()

        @pl.when(k == chunks - 1)
        def _():
            total = jnp.sum(squares[...], axis=2, keepdims=True) * (1.0 / (chunks * width))
            scale_out[...] = jnp.broadcast_to(lax.rsqrt(total + 1e-05), scale_out.shape)
            remote(scale_out, scales.at[core, next_near], 7, scale_recv.at[core, next_near], next_id).start()

    def mid_near_reduce(k):
        w_copy(k).start()
        @pl.when(k == 0)
        def _():
            gain_copy.wait()

        res_copy(k).wait()
        got_copy(k, near, 1, inward_id).wait_recv()
        for sub in range(2):
            sent[near, k, sub] = near_sum(k, sub).astype(BF16)
        got_copy(k, near, 2, outward_id).start()

    def near_spread(k):
        x_copy(k, core, near, 3, inward_id).wait_recv()
        x_copy(k, core, near, 3, inward_id).start()

        @pl.when(k == chunks - 1)
        def _():
            scale_copy(core, near, 8, inward_id).wait_recv()
            scale_copy(core, near, 8, inward_id).start()
            scale_copy(core, near, 9, sibling_id).start()

    def far_spread(k):
        x_copy(k, core, far, 5, outward_id).wait_recv()

        @pl.when(is_mid)
        def _():
            x_copy(k, core, far, 5, outward_id).start()

        both_copy(k).start()

        @pl.when(k == chunks - 1)
        def _():
            scale_copy(core, far, 11, sibling_id).wait_recv()

            @pl.when(is_mid)
            def _():
                scale_copy(core, far, 10, outward_id).start()

            scale_copy(core, far, 11, sibling_id).start()

    def product(k):
        w_copy(k).wait()
        both_copy(k).wait_recv()
        acc[...] += jnp.dot(x[k].reshape(8 * rows, width), wv[k], preferred_element_type=F32)

    @pl.when(is_edge)
    def _():
        @pl.loop(0, chunks + max(EDGE_SKEW))
        def _(i):
            at(i, EDGE_SKEW[0], edge_far_reduce)
            at(i, EDGE_SKEW[1], edge_near_reduce)
            at(i, EDGE_SKEW[2], near_spread)
            at(i, EDGE_SKEW[3], far_spread)
            at(i, EDGE_SKEW[4], product)

    @pl.when(is_mid)
    def _():
        @pl.loop(0, chunks + max(MID_SKEW))
        def _(i):
            at(i, MID_SKEW[0], mid_far_reduce)
            at(i, MID_SKEW[1], mid_near_reduce)
            at(i, MID_SKEW[2], near_spread)
            at(i, MID_SKEW[3], far_spread)
            at(i, MID_SKEW[4], product)

    for flow in range(2):
        scale_copy(1 - core, flow, 9, sibling_id).wait_recv()
    lane_of = (flip_in, 1 - flip_in)
    for of in range(2):
        for flow in range(2):
            for sub in range(2):
                start = (of * 4 + flow * 2 + sub) * rows
                factor = scales[of, flow, sub]
                block = acc[start:start + rows] * jnp.concatenate([factor, factor], axis=1)
                out[lane_of[flow] * 2 + sub, of] = block.astype(BF16)

    def sent_all(ref, kind):
        remote(ref, ref, kind, pair_recv.at[0], sibling_id).wait_send()

    sent_all(down.at[:, 1 - core], 0)
    sent_all(sent.at[far], 1)
    sent_all(sent.at[near], 2)
    sent_all(x.at[:, part(core, near)], 3)
    sent_all(x.at[:, pl.ds(core * 4, 4)], 4)
    sent_all(scales.at[core, near], 8)
    sent_all(scales.at[core, near], 9)
    sent_all(scales.at[core, far], 11)

    @pl.when(is_edge)
    def _():
        sent_all(scale_out, 7)

    @pl.when(is_mid)
    def _():
        sent_all(x.at[:, part(core, far)], 5)
        sent_all(scales.at[core, far], 10)


def body(n_section, down_terms, residual, norm_gain, kv_weight):
    tokens, d = down_terms.shape[2:]
    kv = kv_weight.shape[2]
    rows, chunks = tokens // 8, CHUNKS
    width = d // chunks
    anywhere = pl.BlockSpec(memory_space=pltpu.HBM)
    out = pl.pallas_call(
        functools.partial(kernel, n_section),
        out_shape=jax.ShapeDtypeStruct((4, 2, rows, kv), BF16),
        in_specs=[anywhere] * 4,
        out_specs=pl.BlockSpec(memory_space=pltpu.VMEM),
        scratch_shapes=[
            pltpu.VMEM((chunks, 4, rows, width), BF16),
            pltpu.VMEM((chunks, 4, rows, width), BF16),
            pltpu.VMEM((chunks, rows, width), BF16),
            pltpu.VMEM((1, d), BF16),
            pltpu.VMEM((chunks, width, kv), BF16),
            pltpu.VMEM((2, chunks, 2, rows, width), BF16),
            pltpu.VMEM((2, chunks, 2, rows, width), BF16),
            pltpu.VMEM((chunks, 8, rows, width), BF16),
            pltpu.VMEM((2, rows, 128), F32),
            pltpu.VMEM((2, 2, 2, rows, 128), F32),
            pltpu.VMEM((tokens, kv), F32),
            pltpu.VMEM((2, rows, 128), F32),
            pltpu.SemaphoreType.DMA((chunks,)),
            pltpu.SemaphoreType.DMA((chunks,)),
            pltpu.SemaphoreType.DMA,
            pltpu.SemaphoreType.DMA((chunks,)),
            pltpu.SemaphoreType.DMA((chunks,)),
            pltpu.SemaphoreType.DMA((2, chunks)),
            pltpu.SemaphoreType.DMA((2, chunks)),
            pltpu.SemaphoreType.DMA((chunks,)),
            pltpu.SemaphoreType.DMA((2, 2)),
            pltpu.SemaphoreType.DMA((12,)),
            pltpu.SemaphoreType.REGULAR,
        ],
        compiler_params=pltpu.CompilerParams(
            collective_id=0, has_side_effects=True, vmem_limit_bytes=62 * 1024 * 1024
        ),
        cost_estimate=pl.CostEstimate(flops=2 * tokens * d * kv, bytes_accessed=13 * 2**20, transcendentals=0),
    )(
        down_terms.reshape(4, 2, rows, d),
        residual.reshape(rows, d),
        norm_gain,
        kv_weight.reshape(d, kv),
    )
    return out.reshape(1, tokens, kv)


def solution(mesh):
    in_specs = (
        P("section", "tensor", None, None),
        P("section", "tensor", None),
        P("section", None),
        P("section", None, "tensor"),
    )
    out_specs = P("section", None, "tensor")
    return jax.shard_map(
        functools.partial(body, mesh.shape["section"]), mesh=mesh, in_specs=in_specs, out_specs=out_specs, check_vma=False
    )
```

```python
import functools

import jax
import jax.numpy as jnp
from jax import lax
from jax.experimental import pallas as pl
from jax.experimental.pallas import tpu as pltpu
from jax.sharding import PartitionSpec as P

MESH = pl.DeviceIdType.MESH
BF16, F32 = jnp.bfloat16, jnp.float32

Y_RUN = 4
CHUNKS = 16
EDGE_SKEW = (0, 6, 13, 23, 25)
MID_SKEW = (2, 4, 17, 20, 25)


def kernel(n_section, down, res, gain, weight, out,
           own, pair, resv, gainv, wv, sent, got, x, scale_out, scales, acc, squares,
           load_sem, pair_recv, got_recv, x_recv, sibling_recv, scale_recv, send_sem, line_sem):
    chunks, _, rows, width = pair.shape
    section, tensor = lax.axis_index("section"), lax.axis_index("tensor")
    z, core = tensor // 2, tensor % 2
    near = z // 2
    far = 1 - near
    is_edge = z % 3 == 0
    is_mid = z % 3 != 0
    inward = z + 1 - 2 * near
    outward = z - 1 + 2 * near
    flip_out = (section % Y_RUN) // (Y_RUN - 1)
    flip_in = 1 - (section % Y_RUN + Y_RUN - 1) // Y_RUN
    next_section = (section + 1) % n_section
    prev_section = (section + n_section - 1) % n_section
    next_near = (near + flip_out) % 2

    sibling_id = (section, z * 2 + 1 - core)
    inward_id = (section, inward * 2 + core)
    outward_id = (section, outward * 2 + core)
    next_id = (next_section, next_near * 6 + core)
    prev_id = (prev_section, ((near + flip_in) % 2) * 6 + core)

    def remote(src, dst, kind, recv, device):
        return pltpu.make_async_remote_copy(
            src_ref=src, dst_ref=dst, send_sem=send_sem.at[kind], recv_sem=recv, device_id=device, device_id_type=MESH
        )

    def cols(k):
        return pl.ds(pl.multiple_of(k * width, width), width)

    own_copy = pltpu.make_async_copy(down.at[:, core], own, load_sem.at[0])
    res_copy = pltpu.make_async_copy(res, resv, load_sem.at[1])
    gain_copy = pltpu.make_async_copy(gain, gainv, load_sem.at[2])
    w_copy = pltpu.make_async_copy(weight, wv, load_sem.at[3])

    def pair_copy(k):
        return remote(down.at[:, 1 - core, :, cols(k)], pair.at[k], 0, pair_recv.at[k], sibling_id)

    def got_copy(k, lane, kind, device):
        return remote(sent.at[lane, k], got.at[lane, k], kind, got_recv.at[lane, k], device)

    def part(of, flow):
        return pl.ds(of * 4 + flow * 2, 2)

    def hop_copy(k):
        return remote(sent.at[near, k], x.at[k, part(core, next_near)], 2, x_recv.at[next_near, k], next_id)

    def x_copy(k, of, flow, kind, device):
        return remote(x.at[k, part(of, flow)], x.at[k, part(of, flow)], kind, x_recv.at[flow, k], device)

    def both_copy(k):
        mine = x.at[k, pl.ds(core * 4, 4)]
        return remote(mine, mine, 4, sibling_recv.at[k], sibling_id)

    def scale_copy(of, flow, kind, device):
        return remote(scales.at[of, flow], scales.at[of, flow], kind, scale_recv.at[of, flow], device)

    barrier = pltpu.get_barrier_semaphore()

    def greet(device):
        pl.semaphore_signal(barrier, inc=1, device_id=device, device_id_type=MESH)

    @pl.when(is_edge)
    def _():
        greet(inward_id)
        greet((section, inward * 2 + 1 - core))
        greet(prev_id)

    @pl.when(is_mid)
    def _():
        greet(sibling_id)
        greet(inward_id)

    own_copy.start()
    res_copy.start()
    gain_copy.start()

    @pl.when(is_mid)
    def _():
        pl.semaphore_wait(barrier, 4)
        pl.semaphore_signal(line_sem, inc=1, device_id=outward_id, device_id_type=MESH)

    @pl.when(is_edge)
    def _():
        pl.semaphore_wait(line_sem, 1)

    @pl.loop(0, chunks)
    def _(k):
        pair_copy(k).start()

    w_copy.start()
    acc[...] = jnp.zeros_like(acc)
    squares[...] = jnp.zeros_like(squares)
    own_copy.wait()
    res_copy.wait()
    gain_copy.wait()

    def partial_sum(k, lane, sub):
        index = lane * 2 + sub
        return own[index, :, cols(k)].astype(F32) + pair[k, index].astype(F32)

    def at(i, skew, body):
        k = i - skew

        @pl.when((k >= 0) & (k < chunks))
        def _():
            body(k)

    def arrived(k):
        pair_copy(k).wait_recv()

    def edge_far_reduce(k):
        arrived(k)
        for sub in range(2):
            sent[far, k, sub] = partial_sum(k, far, sub).astype(BF16)
        got_copy(k, far, 1, inward_id).start()

    def mid_far_reduce(k):
        arrived(k)
        got_copy(k, far, 1, inward_id).wait_recv()
        for sub in range(2):
            sent[far, k, sub] = (got[far, k, sub].astype(F32) + partial_sum(k, far, sub)).astype(BF16)
        got_copy(k, far, 1, inward_id).start()

    def near_sum(k, sub):
        mask = ((sub + z + 1) % 2).astype(F32)
        return got[near, k, sub].astype(F32) + partial_sum(k, near, sub) + resv[:, cols(k)].astype(F32) * mask

    def edge_near_reduce(k):
        @pl.when(k == 0)
        def _():
            pl.semaphore_wait(barrier, 1)

        got_copy(k, near, 1, inward_id).wait_recv()
        gain_row = gainv[:, cols(k)].astype(F32)
        for sub in range(2):
            stream = near_sum(k, sub)
            square = stream * stream
            folded = square[:, :128]
            for j in range(1, width // 128):
                folded = folded + square[:, j * 128:(j + 1) * 128]
            squares[sub] += folded
            sent[near, k, sub] = (stream * gain_row).astype(BF16)
        hop_copy(k).start()

        @pl.when(k == chunks - 1)
        def _():
            total = jnp.sum(squares[...], axis=2, keepdims=True) * (1.0 / (chunks * width))
            scale_out[...] = jnp.broadcast_to(lax.rsqrt(total + 1e-05), scale_out.shape)
            remote(scale_out, scales.at[core, next_near], 7, scale_recv.at[core, next_near], next_id).start()

    def mid_near_reduce(k):
        got_copy(k, near, 1, inward_id).wait_recv()
        for sub in range(2):
            sent[near, k, sub] = near_sum(k, sub).astype(BF16)
        got_copy(k, near, 2, outward_id).start()

    def near_spread(k):
        x_copy(k, core, near, 3, inward_id).wait_recv()
        x_copy(k, core, near, 3, inward_id).start()

        @pl.when(k == chunks - 1)
        def _():
            scale_copy(core, near, 8, inward_id).wait_recv()
            scale_copy(core, near, 8, inward_id).start()
            scale_copy(core, near, 9, sibling_id).start()

    def far_spread(k):
        x_copy(k, core, far, 5, outward_id).wait_recv()

        @pl.when(is_mid)
        def _():
            x_copy(k, core, far, 5, outward_id).start()

        both_copy(k).start()

        @pl.when(k == chunks - 1)
        def _():
            scale_copy(core, far, 11, sibling_id).wait_recv()

            @pl.when(is_mid)
            def _():
                scale_copy(core, far, 10, outward_id).start()

            scale_copy(core, far, 11, sibling_id).start()

    def product(k):
        @pl.when(k == 0)
        def _():
            w_copy.wait()

        both_copy(k).wait_recv()
        acc[...] += jnp.dot(x[k].reshape(8 * rows, width), wv[cols(k)], preferred_element_type=F32)

    @pl.when(is_edge)
    def _():
        @pl.loop(0, chunks)
        def _(k):
            edge_far_reduce(k)

        @pl.loop(min(EDGE_SKEW[1:]), chunks + max(EDGE_SKEW))
        def _(i):
            at(i, EDGE_SKEW[1], edge_near_reduce)
            at(i, EDGE_SKEW[2], near_spread)
            at(i, EDGE_SKEW[3], far_spread)
            at(i, EDGE_SKEW[4], product)

    @pl.when(is_mid)
    def _():
        @pl.loop(0, chunks + max(MID_SKEW))
        def _(i):
            at(i, MID_SKEW[0], mid_far_reduce)
            at(i, MID_SKEW[1], mid_near_reduce)
            at(i, MID_SKEW[2], near_spread)
            at(i, MID_SKEW[3], far_spread)
            at(i, MID_SKEW[4], product)

    for flow in range(2):
        scale_copy(1 - core, flow, 9, sibling_id).wait_recv()
    lane_of = (flip_in, 1 - flip_in)
    for of in range(2):
        for flow in range(2):
            for sub in range(2):
                start = (of * 4 + flow * 2 + sub) * rows
                factor = scales[of, flow, sub]
                block = acc[start:start + rows] * jnp.concatenate([factor, factor], axis=1)
                out[lane_of[flow] * 2 + sub, of] = block.astype(BF16)

    def sent_all(ref, kind):
        remote(ref, ref, kind, pair_recv.at[0], sibling_id).wait_send()

    sent_all(down.at[:, 1 - core], 0)
    sent_all(sent.at[far], 1)
    sent_all(sent.at[near], 2)
    sent_all(x.at[:, part(core, near)], 3)
    sent_all(x.at[:, pl.ds(core * 4, 4)], 4)
    sent_all(scales.at[core, near], 8)
    sent_all(scales.at[core, near], 9)
    sent_all(scales.at[core, far], 11)

    @pl.when(is_edge)
    def _():
        sent_all(scale_out, 7)

    @pl.when(is_mid)
    def _():
        sent_all(x.at[:, part(core, far)], 5)
        sent_all(scales.at[core, far], 10)


def body(n_section, down_terms, residual, norm_gain, kv_weight):
    tokens, d = down_terms.shape[2:]
    kv = kv_weight.shape[2]
    rows, chunks = tokens // 8, CHUNKS
    width = d // chunks
    anywhere = pl.BlockSpec(memory_space=pltpu.HBM)
    out = pl.pallas_call(
        functools.partial(kernel, n_section),
        out_shape=jax.ShapeDtypeStruct((4, 2, rows, kv), BF16),
        in_specs=[anywhere] * 4,
        out_specs=pl.BlockSpec(memory_space=pltpu.VMEM),
        scratch_shapes=[
            pltpu.VMEM((4, rows, d), BF16),
            pltpu.VMEM((chunks, 4, rows, width), BF16),
            pltpu.VMEM((rows, d), BF16),
            pltpu.VMEM((1, d), BF16),
            pltpu.VMEM((d, kv), BF16),
            pltpu.VMEM((2, chunks, 2, rows, width), BF16),
            pltpu.VMEM((2, chunks, 2, rows, width), BF16),
            pltpu.VMEM((chunks, 8, rows, width), BF16),
            pltpu.VMEM((2, rows, 128), F32),
            pltpu.VMEM((2, 2, 2, rows, 128), F32),
            pltpu.VMEM((tokens, kv), F32),
            pltpu.VMEM((2, rows, 128), F32),
            pltpu.SemaphoreType.DMA((4,)),
            pltpu.SemaphoreType.DMA((chunks,)),
            pltpu.SemaphoreType.DMA((2, chunks)),
            pltpu.SemaphoreType.DMA((2, chunks)),
            pltpu.SemaphoreType.DMA((chunks,)),
            pltpu.SemaphoreType.DMA((2, 2)),
            pltpu.SemaphoreType.DMA((12,)),
            pltpu.SemaphoreType.REGULAR,
        ],
        compiler_params=pltpu.CompilerParams(
            collective_id=0, has_side_effects=True, vmem_limit_bytes=62 * 1024 * 1024
        ),
        cost_estimate=pl.CostEstimate(flops=2 * tokens * d * kv, bytes_accessed=13 * 2**20, transcendentals=0),
    )(
        down_terms.reshape(4, 2, rows, d),
        residual.reshape(rows, d),
        norm_gain,
        kv_weight.reshape(d, kv),
    )
    return out.reshape(1, tokens, kv)


def solution(mesh):
    in_specs = (
        P("section", "tensor", None, None),
        P("section", "tensor", None),
        P("section", None),
        P("section", None, "tensor"),
    )
    out_specs = P("section", None, "tensor")
    return jax.shard_map(
        functools.partial(body, mesh.shape["section"]), mesh=mesh, in_specs=in_specs, out_specs=out_specs, check_vma=False
    )
```

```python
import functools

import jax
import jax.numpy as jnp
from jax import lax
from jax.experimental import pallas as pl
from jax.experimental.pallas import tpu as pltpu
from jax.sharding import PartitionSpec as P

MESH = pl.DeviceIdType.MESH
BF16, F32 = jnp.bfloat16, jnp.float32

Y_RUN = 4
CHUNKS = 32
EDGE_SKEW = (0, 12, 28, 42, 44)
MID_SKEW = (4, 8, 35, 40, 44)


def kernel(n_section, down, res, gain, weight, out,
           own, pair, resv, gainv, wv, sent, got, x, scale_out, scales, acc, squares,
           load_sem, pair_recv, got_recv, x_recv, sibling_recv, scale_recv, send_sem, line_sem):
    chunks, _, rows, width = pair.shape
    section, tensor = lax.axis_index("section"), lax.axis_index("tensor")
    z, core = tensor // 2, tensor % 2
    near = z // 2
    far = 1 - near
    is_edge = z % 3 == 0
    is_mid = z % 3 != 0
    inward = z + 1 - 2 * near
    outward = z - 1 + 2 * near
    flip_out = (section % Y_RUN) // (Y_RUN - 1)
    flip_in = 1 - (section % Y_RUN + Y_RUN - 1) // Y_RUN
    next_section = (section + 1) % n_section
    prev_section = (section + n_section - 1) % n_section
    next_near = (near + flip_out) % 2

    sibling_id = (section, z * 2 + 1 - core)
    inward_id = (section, inward * 2 + core)
    outward_id = (section, outward * 2 + core)
    next_id = (next_section, next_near * 6 + core)
    prev_id = (prev_section, ((near + flip_in) % 2) * 6 + core)

    def remote(src, dst, kind, recv, device):
        return pltpu.make_async_remote_copy(
            src_ref=src, dst_ref=dst, send_sem=send_sem.at[kind], recv_sem=recv, device_id=device, device_id_type=MESH
        )

    def cols(k):
        return pl.ds(pl.multiple_of(k * width, width), width)

    own_copy = pltpu.make_async_copy(down.at[:, core], own, load_sem.at[0])
    res_copy = pltpu.make_async_copy(res, resv, load_sem.at[1])
    gain_copy = pltpu.make_async_copy(gain, gainv, load_sem.at[2])
    w_copy = pltpu.make_async_copy(weight, wv, load_sem.at[3])

    def pair_copy(k):
        return remote(down.at[:, 1 - core, :, cols(k)], pair.at[k], 0, pair_recv.at[k], sibling_id)

    def got_copy(k, lane, kind, device):
        return remote(sent.at[lane, k], got.at[lane, k], kind, got_recv.at[lane, k], device)

    def part(of, flow):
        return pl.ds(of * 4 + flow * 2, 2)

    def hop_copy(k):
        return remote(sent.at[near, k], x.at[k, part(core, next_near)], 2, x_recv.at[next_near, k], next_id)

    def x_copy(k, of, flow, kind, device):
        return remote(x.at[k, part(of, flow)], x.at[k, part(of, flow)], kind, x_recv.at[flow, k], device)

    def both_copy(k):
        mine = x.at[k, pl.ds(core * 4, 4)]
        return remote(mine, mine, 4, sibling_recv.at[k], sibling_id)

    def scale_copy(of, flow, kind, device):
        return remote(scales.at[of, flow], scales.at[of, flow], kind, scale_recv.at[of, flow], device)

    barrier = pltpu.get_barrier_semaphore()

    def greet(device):
        pl.semaphore_signal(barrier, inc=1, device_id=device, device_id_type=MESH)

    @pl.when(is_edge)
    def _():
        greet(inward_id)
        greet((section, inward * 2 + 1 - core))
        greet(prev_id)

    @pl.when(is_mid)
    def _():
        greet(sibling_id)
        greet(inward_id)

    own_copy.start()
    res_copy.start()
    gain_copy.start()

    @pl.when(is_mid)
    def _():
        pl.semaphore_wait(barrier, 4)
        pl.semaphore_signal(line_sem, inc=1, device_id=outward_id, device_id_type=MESH)

    @pl.when(is_edge)
    def _():
        pl.semaphore_wait(line_sem, 1)

    @pl.loop(0, chunks)
    def _(k):
        pair_copy(k).start()

    w_copy.start()
    acc[...] = jnp.zeros_like(acc)
    squares[...] = jnp.zeros_like(squares)
    own_copy.wait()
    res_copy.wait()
    gain_copy.wait()

    def partial_sum(k, lane, sub):
        index = lane * 2 + sub
        return own[index, :, cols(k)].astype(F32) + pair[k, index].astype(F32)

    def at(i, skew, body):
        k = i - skew

        @pl.when((k >= 0) & (k < chunks))
        def _():
            body(k)

    def arrived(k):
        pair_copy(k).wait_recv()

    def edge_far_reduce(k):
        arrived(k)
        for sub in range(2):
            sent[far, k, sub] = partial_sum(k, far, sub).astype(BF16)
        got_copy(k, far, 1, inward_id).start()

    def mid_far_reduce(k):
        arrived(k)
        got_copy(k, far, 1, inward_id).wait_recv()
        for sub in range(2):
            sent[far, k, sub] = (got[far, k, sub].astype(F32) + partial_sum(k, far, sub)).astype(BF16)
        got_copy(k, far, 1, inward_id).start()

    def near_sum(k, sub):
        mask = ((sub + z + 1) % 2).astype(F32)
        return got[near, k, sub].astype(F32) + partial_sum(k, near, sub) + resv[:, cols(k)].astype(F32) * mask

    def edge_near_reduce(k):
        @pl.when(k == 0)
        def _():
            pl.semaphore_wait(barrier, 1)

        got_copy(k, near, 1, inward_id).wait_recv()
        gain_row = gainv[:, cols(k)].astype(F32)
        for sub in range(2):
            stream = near_sum(k, sub)
            square = stream * stream
            folded = square[:, :128]
            for j in range(1, width // 128):
                folded = folded + square[:, j * 128:(j + 1) * 128]
            squares[sub] += folded
            sent[near, k, sub] = (stream * gain_row).astype(BF16)
        hop_copy(k).start()

        @pl.when(k == chunks - 1)
        def _():
            total = jnp.sum(squares[...], axis=2, keepdims=True) * (1.0 / (chunks * width))
            scale_out[...] = jnp.broadcast_to(lax.rsqrt(total + 1e-05), scale_out.shape)
            remote(scale_out, scales.at[core, next_near], 7, scale_recv.at[core, next_near], next_id).start()

    def mid_near_reduce(k):
        got_copy(k, near, 1, inward_id).wait_recv()
        for sub in range(2):
            sent[near, k, sub] = near_sum(k, sub).astype(BF16)
        got_copy(k, near, 2, outward_id).start()

    def near_spread(k):
        x_copy(k, core, near, 3, inward_id).wait_recv()
        x_copy(k, core, near, 3, inward_id).start()

        @pl.when(k == chunks - 1)
        def _():
            scale_copy(core, near, 8, inward_id).wait_recv()
            scale_copy(core, near, 8, inward_id).start()
            scale_copy(core, near, 9, sibling_id).start()

    def far_spread(k):
        x_copy(k, core, far, 5, outward_id).wait_recv()

        @pl.when(is_mid)
        def _():
            x_copy(k, core, far, 5, outward_id).start()

        both_copy(k).start()

        @pl.when(k == chunks - 1)
        def _():
            scale_copy(core, far, 11, sibling_id).wait_recv()

            @pl.when(is_mid)
            def _():
                scale_copy(core, far, 10, outward_id).start()

            scale_copy(core, far, 11, sibling_id).start()

    def product(k):
        @pl.when(k == 0)
        def _():
            w_copy.wait()

        both_copy(k).wait_recv()
        acc[...] += jnp.dot(x[k].reshape(8 * rows, width), wv[cols(k)], preferred_element_type=F32)

    @pl.when(is_edge)
    def _():
        @pl.loop(0, chunks)
        def _(k):
            edge_far_reduce(k)

        @pl.loop(min(EDGE_SKEW[1:]), chunks + max(EDGE_SKEW))
        def _(i):
            at(i, EDGE_SKEW[1], edge_near_reduce)
            at(i, EDGE_SKEW[2], near_spread)
            at(i, EDGE_SKEW[3], far_spread)
            at(i, EDGE_SKEW[4], product)

    @pl.when(is_mid)
    def _():
        @pl.loop(0, chunks + max(MID_SKEW))
        def _(i):
            at(i, MID_SKEW[0], mid_far_reduce)
            at(i, MID_SKEW[1], mid_near_reduce)
            at(i, MID_SKEW[2], near_spread)
            at(i, MID_SKEW[3], far_spread)
            at(i, MID_SKEW[4], product)

    for flow in range(2):
        scale_copy(1 - core, flow, 9, sibling_id).wait_recv()
    lane_of = (flip_in, 1 - flip_in)
    for of in range(2):
        for flow in range(2):
            for sub in range(2):
                start = (of * 4 + flow * 2 + sub) * rows
                factor = scales[of, flow, sub]
                block = acc[start:start + rows] * jnp.concatenate([factor, factor], axis=1)
                out[lane_of[flow] * 2 + sub, of] = block.astype(BF16)

    def sent_all(ref, kind):
        remote(ref, ref, kind, pair_recv.at[0], sibling_id).wait_send()

    sent_all(down.at[:, 1 - core], 0)
    sent_all(sent.at[far], 1)
    sent_all(sent.at[near], 2)
    sent_all(x.at[:, part(core, near)], 3)
    sent_all(x.at[:, pl.ds(core * 4, 4)], 4)
    sent_all(scales.at[core, near], 8)
    sent_all(scales.at[core, near], 9)
    sent_all(scales.at[core, far], 11)

    @pl.when(is_edge)
    def _():
        sent_all(scale_out, 7)

    @pl.when(is_mid)
    def _():
        sent_all(x.at[:, part(core, far)], 5)
        sent_all(scales.at[core, far], 10)


def body(n_section, down_terms, residual, norm_gain, kv_weight):
    tokens, d = down_terms.shape[2:]
    kv = kv_weight.shape[2]
    rows, chunks = tokens // 8, CHUNKS
    width = d // chunks
    anywhere = pl.BlockSpec(memory_space=pltpu.HBM)
    out = pl.pallas_call(
        functools.partial(kernel, n_section),
        out_shape=jax.ShapeDtypeStruct((4, 2, rows, kv), BF16),
        in_specs=[anywhere] * 4,
        out_specs=pl.BlockSpec(memory_space=pltpu.VMEM),
        scratch_shapes=[
            pltpu.VMEM((4, rows, d), BF16),
            pltpu.VMEM((chunks, 4, rows, width), BF16),
            pltpu.VMEM((rows, d), BF16),
            pltpu.VMEM((1, d), BF16),
            pltpu.VMEM((d, kv), BF16),
            pltpu.VMEM((2, chunks, 2, rows, width), BF16),
            pltpu.VMEM((2, chunks, 2, rows, width), BF16),
            pltpu.VMEM((chunks, 8, rows, width), BF16),
            pltpu.VMEM((2, rows, 128), F32),
            pltpu.VMEM((2, 2, 2, rows, 128), F32),
            pltpu.VMEM((tokens, kv), F32),
            pltpu.VMEM((2, rows, 128), F32),
            pltpu.SemaphoreType.DMA((4,)),
            pltpu.SemaphoreType.DMA((chunks,)),
            pltpu.SemaphoreType.DMA((2, chunks)),
            pltpu.SemaphoreType.DMA((2, chunks)),
            pltpu.SemaphoreType.DMA((chunks,)),
            pltpu.SemaphoreType.DMA((2, 2)),
            pltpu.SemaphoreType.DMA((12,)),
            pltpu.SemaphoreType.REGULAR,
        ],
        compiler_params=pltpu.CompilerParams(
            collective_id=0, has_side_effects=True, vmem_limit_bytes=40 * 1024 * 1024
        ),
        cost_estimate=pl.CostEstimate(flops=2 * tokens * d * kv, bytes_accessed=13 * 2**20, transcendentals=0),
    )(*(
        pltpu.with_memory_space_constraint(array, pltpu.HBM)
        for array in (down_terms.reshape(4, 2, rows, d), residual.reshape(rows, d), norm_gain, kv_weight.reshape(d, kv))
    ))
    return out.reshape(1, tokens, kv)


def solution(mesh):
    in_specs = (
        P("section", "tensor", None, None),
        P("section", "tensor", None),
        P("section", None),
        P("section", None, "tensor"),
    )
    out_specs = P("section", None, "tensor")
    return jax.shard_map(
        functools.partial(body, mesh.shape["section"]), mesh=mesh, in_specs=in_specs, out_specs=out_specs, check_vma=False
    )
```

```python
import functools

import jax
import jax.numpy as jnp
from jax import lax
from jax.experimental import pallas as pl
from jax.experimental.pallas import tpu as pltpu
from jax.sharding import PartitionSpec as P

MESH = pl.DeviceIdType.MESH
BF16, F32 = jnp.bfloat16, jnp.float32

Y_RUN = 4
CHUNKS = 32
EDGE_SKEW = (0, 12, 28, 42, 44)
MID_SKEW = (4, 8, 35, 40, 44)


def kernel(n_section, down, res, gain, weight, out,
           own, pair, resv, gainv, wv, sent, got, x, scale_out, scales, acc, squares,
           load_sem, pair_recv, got_recv, x_recv, sibling_recv, scale_recv, send_sem, line_sem):
    chunks, _, rows, width = pair.shape
    section, tensor = lax.axis_index("section"), lax.axis_index("tensor")
    z, core = tensor // 2, tensor % 2
    near = z // 2
    far = 1 - near
    is_edge = z % 3 == 0
    is_mid = z % 3 != 0
    inward = z + 1 - 2 * near
    outward = z - 1 + 2 * near
    flip_out = (section % Y_RUN) // (Y_RUN - 1)
    flip_in = 1 - (section % Y_RUN + Y_RUN - 1) // Y_RUN
    next_section = (section + 1) % n_section
    prev_section = (section + n_section - 1) % n_section
    next_near = (near + flip_out) % 2

    sibling_id = (section, z * 2 + 1 - core)
    inward_id = (section, inward * 2 + core)
    outward_id = (section, outward * 2 + core)
    next_id = (next_section, next_near * 6 + core)
    prev_id = (prev_section, ((near + flip_in) % 2) * 6 + core)

    def remote(src, dst, kind, recv, device):
        return pltpu.make_async_remote_copy(
            src_ref=src, dst_ref=dst, send_sem=send_sem.at[kind], recv_sem=recv, device_id=device, device_id_type=MESH
        )

    def cols(k):
        return pl.ds(pl.multiple_of(k * width, width), width)

    own_copy = pltpu.make_async_copy(down.at[:, core], own, load_sem.at[0])
    res_copy = pltpu.make_async_copy(res, resv, load_sem.at[1])
    gain_copy = pltpu.make_async_copy(gain, gainv, load_sem.at[2])
    w_copy = pltpu.make_async_copy(weight, wv, load_sem.at[3])

    def pair_copy(k):
        return remote(down.at[:, 1 - core, :, cols(k)], pair.at[k], 0, pair_recv.at[k], sibling_id)

    def got_copy(k, lane, kind, device):
        return remote(sent.at[lane, k], got.at[lane, k], kind, got_recv.at[lane, k], device)

    def part(of, flow):
        return pl.ds(of * 4 + flow * 2, 2)

    def hop_copy(k):
        return remote(sent.at[near, k], x.at[k, part(core, next_near)], 2, x_recv.at[next_near, k], next_id)

    def x_copy(k, of, flow, kind, device):
        return remote(x.at[k, part(of, flow)], x.at[k, part(of, flow)], kind, x_recv.at[flow, k], device)

    def both_copy(k):
        mine = x.at[k, pl.ds(core * 4, 4)]
        return remote(mine, mine, 4, sibling_recv.at[k], sibling_id)

    def scale_copy(of, flow, kind, device):
        return remote(scales.at[of, flow], scales.at[of, flow], kind, scale_recv.at[of, flow], device)

    barrier = pltpu.get_barrier_semaphore()

    def greet(device):
        pl.semaphore_signal(barrier, inc=1, device_id=device, device_id_type=MESH)

    @pl.when(is_edge)
    def _():
        greet(inward_id)
        greet((section, inward * 2 + 1 - core))
        greet(prev_id)

    @pl.when(is_mid)
    def _():
        greet(sibling_id)
        greet(inward_id)

    own_copy.start()
    res_copy.start()
    gain_copy.start()

    @pl.when(is_mid)
    def _():
        pl.semaphore_wait(barrier, 4)
        pl.semaphore_signal(line_sem, inc=1, device_id=outward_id, device_id_type=MESH)

    @pl.when(is_edge)
    def _():
        pl.semaphore_wait(line_sem, 1)

    @pl.loop(0, chunks)
    def _(k):
        pair_copy(k).start()

    w_copy.start()
    acc[...] = jnp.zeros_like(acc)
    squares[...] = jnp.zeros_like(squares)
    own_copy.wait()
    res_copy.wait()
    gain_copy.wait()

    def partial_sum(k, lane, sub):
        index = lane * 2 + sub
        return own[index, :, cols(k)].astype(F32) + pair[k, index].astype(F32)

    def at(i, skew, body):
        k = i - skew

        @pl.when((k >= 0) & (k < chunks))
        def _():
            body(k)

    def arrived(k):
        pair_copy(k).wait_recv()

    def edge_far_reduce(k):
        arrived(k)
        for sub in range(2):
            sent[far, k, sub] = partial_sum(k, far, sub).astype(BF16)
        got_copy(k, far, 1, inward_id).start()

    def mid_far_reduce(k):
        arrived(k)
        got_copy(k, far, 1, inward_id).wait_recv()
        for sub in range(2):
            sent[far, k, sub] = (got[far, k, sub].astype(F32) + partial_sum(k, far, sub)).astype(BF16)
        got_copy(k, far, 1, inward_id).start()

    def near_sum(k, sub):
        mask = ((sub + z + 1) % 2).astype(F32)
        return got[near, k, sub].astype(F32) + partial_sum(k, near, sub) + resv[:, cols(k)].astype(F32) * mask

    def edge_near_reduce(k):
        @pl.when(k == 0)
        def _():
            pl.semaphore_wait(barrier, 1)

        got_copy(k, near, 1, inward_id).wait_recv()
        gain_row = gainv[:, cols(k)].astype(F32)
        for sub in range(2):
            stream = near_sum(k, sub)
            square = stream * stream
            folded = square[:, :128]
            for j in range(1, width // 128):
                folded = folded + square[:, j * 128:(j + 1) * 128]
            squares[sub] += folded
            sent[near, k, sub] = (stream * gain_row).astype(BF16)
        hop_copy(k).start()

        @pl.when(k == chunks - 1)
        def _():
            total = jnp.sum(squares[...], axis=2, keepdims=True) * (1.0 / (chunks * width))
            scale_out[...] = jnp.broadcast_to(lax.rsqrt(total + 1e-05), scale_out.shape)
            remote(scale_out, scales.at[core, next_near], 7, scale_recv.at[core, next_near], next_id).start()

    def mid_near_reduce(k):
        got_copy(k, near, 1, inward_id).wait_recv()
        for sub in range(2):
            sent[near, k, sub] = near_sum(k, sub).astype(BF16)
        got_copy(k, near, 2, outward_id).start()

    def near_spread(k):
        x_copy(k, core, near, 3, inward_id).wait_recv()
        x_copy(k, core, near, 3, inward_id).start()

        @pl.when(k == chunks - 1)
        def _():
            scale_copy(core, near, 8, inward_id).wait_recv()
            scale_copy(core, near, 8, inward_id).start()
            scale_copy(core, near, 9, sibling_id).start()

    def far_spread(k):
        x_copy(k, core, far, 5, sibling_id).wait_recv()

        @pl.when(is_mid)
        def _():
            x_copy(k, core, far, 5, outward_id).start()

        both_copy(k).start()

        @pl.when(k == chunks - 1)
        def _():
            scale_copy(core, far, 11, sibling_id).wait_recv()

            @pl.when(is_mid)
            def _():
                scale_copy(core, far, 10, outward_id).start()

            scale_copy(core, far, 11, sibling_id).start()

    def product(k):
        @pl.when(k == 0)
        def _():
            w_copy.wait()

        both_copy(k).wait_recv()
        acc[...] += jnp.dot(x[k].reshape(8 * rows, width), wv[cols(k)], preferred_element_type=F32)

    @pl.when(is_edge)
    def _():
        @pl.loop(0, chunks)
        def _(k):
            edge_far_reduce(k)

        @pl.loop(min(EDGE_SKEW[1:]), chunks + max(EDGE_SKEW))
        def _(i):
            at(i, EDGE_SKEW[1], edge_near_reduce)
            at(i, EDGE_SKEW[2], near_spread)
            at(i, EDGE_SKEW[3], far_spread)
            at(i, EDGE_SKEW[4], product)

    @pl.when(is_mid)
    def _():
        @pl.loop(0, chunks + max(MID_SKEW))
        def _(i):
            at(i, MID_SKEW[0], mid_far_reduce)
            at(i, MID_SKEW[1], mid_near_reduce)
            at(i, MID_SKEW[2], near_spread)
            at(i, MID_SKEW[3], far_spread)
            at(i, MID_SKEW[4], product)

    for flow in range(2):
        scale_copy(1 - core, flow, 9, sibling_id).wait_recv()
    lane_of = (flip_in, 1 - flip_in)
    for of in range(2):
        for flow in range(2):
            for sub in range(2):
                start = (of * 4 + flow * 2 + sub) * rows
                factor = scales[of, flow, sub]
                block = acc[start:start + rows] * jnp.concatenate([factor, factor], axis=1)
                out[lane_of[flow] * 2 + sub, of] = block.astype(BF16)

    def sent_all(ref, kind):
        remote(ref, ref, kind, pair_recv.at[0], sibling_id).wait_send()

    sent_all(down.at[:, 1 - core], 0)
    sent_all(sent.at[far], 1)
    sent_all(sent.at[near], 2)
    sent_all(x.at[:, part(core, near)], 3)
    sent_all(x.at[:, pl.ds(core * 4, 4)], 4)
    sent_all(scales.at[core, near], 8)
    sent_all(scales.at[core, near], 9)
    sent_all(scales.at[core, far], 11)

    @pl.when(is_edge)
    def _():
        sent_all(scale_out, 7)

    @pl.when(is_mid)
    def _():
        sent_all(x.at[:, part(core, far)], 5)
        sent_all(scales.at[core, far], 10)


def body(n_section, down_terms, residual, norm_gain, kv_weight):
    tokens, d = down_terms.shape[2:]
    kv = kv_weight.shape[2]
    rows, chunks = tokens // 8, CHUNKS
    width = d // chunks
    anywhere = pl.BlockSpec(memory_space=pltpu.HBM)
    out = pl.pallas_call(
        functools.partial(kernel, n_section),
        out_shape=jax.ShapeDtypeStruct((4, 2, rows, kv), BF16),
        in_specs=[anywhere] * 4,
        out_specs=pl.BlockSpec(memory_space=pltpu.VMEM),
        scratch_shapes=[
            pltpu.VMEM((4, rows, d), BF16),
            pltpu.VMEM((chunks, 4, rows, width), BF16),
            pltpu.VMEM((rows, d), BF16),
            pltpu.VMEM((1, d), BF16),
            pltpu.VMEM((d, kv), BF16),
            pltpu.VMEM((2, chunks, 2, rows, width), BF16),
            pltpu.VMEM((2, chunks, 2, rows, width), BF16),
            pltpu.VMEM((chunks, 8, rows, width), BF16),
            pltpu.VMEM((2, rows, 128), F32),
            pltpu.VMEM((2, 2, 2, rows, 128), F32),
            pltpu.VMEM((tokens, kv), F32),
            pltpu.VMEM((2, rows, 128), F32),
            pltpu.SemaphoreType.DMA((4,)),
            pltpu.SemaphoreType.DMA((chunks,)),
            pltpu.SemaphoreType.DMA((2, chunks)),
            pltpu.SemaphoreType.DMA((2, chunks)),
            pltpu.SemaphoreType.DMA((chunks,)),
            pltpu.SemaphoreType.DMA((2, 2)),
            pltpu.SemaphoreType.DMA((12,)),
            pltpu.SemaphoreType.REGULAR,
        ],
        compiler_params=pltpu.CompilerParams(
            collective_id=0, has_side_effects=True, vmem_limit_bytes=40 * 1024 * 1024
        ),
        cost_estimate=pl.CostEstimate(flops=2 * tokens * d * kv, bytes_accessed=13 * 2**20, transcendentals=0),
    )(*(
        pltpu.with_memory_space_constraint(array, pltpu.HBM)
        for array in (down_terms.reshape(4, 2, rows, d), residual.reshape(rows, d), norm_gain, kv_weight.reshape(d, kv))
    ))
    return out.reshape(1, tokens, kv)


def solution(mesh):
    in_specs = (
        P("section", "tensor", None, None),
        P("section", "tensor", None),
        P("section", None),
        P("section", None, "tensor"),
    )
    out_specs = P("section", None, "tensor")
    return jax.shard_map(
        functools.partial(body, mesh.shape["section"]), mesh=mesh, in_specs=in_specs, out_specs=out_specs, check_vma=False
    )
```
